32 devices in a mesh: ax: 4 (over y, x), ay: 8 (over z, core).
Axes of the slice: x: 2, y: 2, z: 4, core: 2. Of those that a mesh axis runs over, the one named last changes fastest.
Arguments:
- noise: float32 [16, 1024, 2048], P(None, ('ax', 'ay')), may hold values from -6 to 6
- kappa: float32 [16, 1024, 2048], P(None, 'ax', 'ay'), may hold values from 0.05 to 2
- mask: int32 [1024, 2048], P('ax', 'ay'), may hold values 0 or 1
Outputs:
- sample: float32 [16, 1024, 2048], P(None, 'ax', 'ay')
The draws below stay inside these ranges and needn't reach their ends.
All inputs are finite; a program needn't handle non-finite values. No bound on the sum of `mask` on one device may be relied on, other than what follows from the above.
Results may differ from the reference program's by a relative error of at most 0.00002.
Values sent between devices are 32-bit elements; how exact they have to be, the bound alone decides.
No kernel may reach another device: no remote copies, remote signals or barrier semaphores. Data moves between devices by JAX's collectives and lax.ppermute only.
A program may use at most 128 MiB of HBM per device.

```python
import math
import jax
import jax.numpy as jnp

NZ = 16
NX = 1024
NY = 2048


def touch_ends(values, stream_key, low, top_value):
    extent = values.shape
    index_at = [jax.random.randint(jax.random.fold_in(stream_key, axis), (), 0, extent[axis]) for axis in range(len(extent))]
    values = values.at[tuple(index_at)].set(low)
    longest = extent.index(max(extent))
    index_at[longest] = (index_at[longest] + 1) % extent[longest]
    return values.at[tuple(index_at)].set(top_value)


def block_scale(key, dims, split, smallest, high):
    def one(dim, shards_of):
        draws = jax.random.uniform(jax.random.fold_in(jax.random.fold_in(key, 6), dim), (shards_of,), jnp.float32, smallest / len(split), high / len(split))
        return jnp.repeat(jnp.exp(draws), dims[dim] // shards_of).reshape((-1,) + (1,) * (len(dims) - dim - 1))

    gain = one(*split[0])
    for cut in split[1:]:
        gain = gain * one(*cut)
    return gain


def centred(own_key, extent, deviation, most, cuts=(), kind=jnp.bfloat16):
    entries = jax.random.normal(own_key, extent, jnp.float32) * deviation
    if len(cuts) > 0:
        entries = block_scale(own_key, extent, cuts, -0.22, 0.18) * entries
    return jnp.clip(entries, min=-most, max=most).astype(kind)


def setup_inputs(seed: int = 0) -> dict:
    arg_keys = jax.random.split(jax.random.key(seed), 4)
    return {
        "noise": centred(arg_keys[0], (NZ, NX, NY), 1.0, 6.0, ((1, 32),), jnp.float32),
        "kappa": jnp.clip(jnp.exp(math.log(2.0) - 3.6888794 * jax.random.uniform(arg_keys[1], (NZ, NX, NY), jnp.float32) ** block_scale(arg_keys[1], (NZ, NX, NY), ((1, 4), (2, 8)), -0.2, 0.2)), 0.05, 2.0),
        "mask": touch_ends((jax.random.randint(arg_keys[2], (NX, NY), 0, 4) < 3).astype(jnp.int32), jax.random.fold_in(arg_keys[2], 1), 0, 1),
    }


def neighbours(padded):
    centre = padded[:, 1:-1, 1:-1]
    with_ends = jnp.pad(centre, ((1, 1), (0, 0), (0, 0)))
    total = padded[:, 2:, 1:-1] + padded[:, :-2, 1:-1]
    total = total + padded[:, 1:-1, 2:] + padded[:, 1:-1, :-2]
    return total + with_ends[2:] + with_ends[:-2]


def factors(kappa):
    pivots = []
    for layer_index in range(kappa.shape[0]):
        diagonal = 2.5 + kappa[layer_index]
        if layer_index > 0:
            diagonal = diagonal - pivots[-1]
        pivots.append(1.0 / diagonal)
    return pivots


def thomas(field, pivots):
    layers = field.shape[0]
    forward = []
    for layer_index in range(layers):
        current = field[layer_index]
        if layer_index > 0:
            current = current + forward[-1]
        forward.append(current * pivots[layer_index])
    result = [None] * layers
    solved = forward[layers - 1]
    result[layers - 1] = solved
    for layer_index in range(layers - 2, -1, -1):
        solved = forward[layer_index] + pivots[layer_index] * solved
        result[layer_index] = solved
    return jnp.stack(result, 0)


def reference(noise, kappa, mask):
    inverse = mask[None].astype(jnp.float32) / (6.0 + kappa)
    field = inverse * noise
    for repeat in range(2):
        padded = jnp.pad(field, ((0, 0), (1, 1), (1, 1)))
        field = inverse * (noise + neighbours(padded))
    return thomas(field, factors(kappa))
```

```python
import functools

import jax
import jax.numpy as jnp
from jax import lax
from jax.experimental import pallas as pl
from jax.experimental.pallas import tpu as pltpu
from jax.sharding import PartitionSpec as P

LANES = 128
SLOT = 8
GROUP = 8


def lanes_of(rows):
    return lax.broadcasted_iota(jnp.int32, (rows, LANES), 1)


def pack_kernel(cells, out):
    layers, rows, columns = cells.shape
    lane = lanes_of(rows)

    def step(layer, packed):
        both = jnp.where(lane < LANES // 2, cells[layer, :, :LANES], cells[layer, :, columns - LANES :])
        return jnp.where(lane // SLOT == layer, pltpu.roll(both, layer * SLOT + 4, 1), packed)

    out[...] = lax.fori_loop(0, layers, step, jnp.zeros((rows, LANES), jnp.float32))


def pack(cells, columns, rows):
    layers, height, width = cells.shape
    return pl.pallas_call(
        pack_kernel,
        grid=(width // columns, height // rows),
        in_specs=[pl.BlockSpec((layers, rows, columns), lambda b, r: (0, r, b))],
        out_specs=pl.BlockSpec((None, rows, LANES), lambda b, r: (b, r, 0)),
        out_shape=jax.ShapeDtypeStruct((width // columns, height, LANES), jnp.float32),
    )(cells)


def around(cells, sides, layer, first, rows):
    tiles = cells.shape[1]
    lane = lanes_of(rows)
    side = pltpu.roll(sides, LANES - 3 - layer * SLOT, 1)
    centre = [cells[layer + 1, t, pl.ds(first, rows), :] for t in range(tiles)]
    left = [pltpu.roll(x, 1, 1) for x in centre]
    right = [pltpu.roll(x, LANES - 1, 1) for x in centre]
    totals = []
    for t in range(tiles):
        total = cells[layer + 1, t, pl.ds(first + 1, rows), :] + cells[layer + 1, t, pl.ds(first - 1, rows), :]
        total = total + jnp.where(lane == 0, side if t == 0 else left[t - 1], left[t])
        total = total + jnp.where(lane == LANES - 1, side if t == tiles - 1 else right[t + 1], right[t])
        totals.append(total + cells[layer, t, pl.ds(first, rows), :] + cells[layer + 2, t, pl.ds(first, rows), :])
    return totals


def window_kernel(half, is_far, *refs):
    if is_far:
        inverse_in, pivots_in, packed_noise, packed_inverse, near, end, *pieces = refs[: 6 + half]
        rest = refs[7 + half :]
    else:
        inverse_in, pivots_in, packed_noise, packed_inverse, near = refs[:5]
        rest = refs[5:]
    out, noise, inverse, pivots, initial, middle, forward, result, sems, out_sems = rest
    layers, groups, _, columns = pivots.shape
    tiles = columns // LANES
    span = groups + 2
    rows, kept = span * GROUP, groups * GROUP
    me = lax.axis_index("ay")
    upper = me // half
    if is_far:
        start = (groups - 2) * (1 - upper)
        depth = pieces[0].shape[1]
        copies = [
            pltpu.make_async_copy(near, noise.at[:, pl.ds((span - 2) * upper, 2)], sems.at[2]),
            pltpu.make_async_copy(end, noise.at[:, pl.ds((span - 1) * (1 - upper), 1)], sems.at[3]),
        ]
        for i, piece in enumerate(pieces):
            place = 2 - upper + depth * ((me % half) ^ (half - 1 - i))
            copies.append(pltpu.make_async_copy(piece, noise.at[:, pl.ds(place, depth)], sems.at[4 + i]))
    else:
        start = (groups + 2) * upper
        copies = [pltpu.make_async_copy(near, noise, sems.at[2])]
    copies.append(pltpu.make_async_copy(inverse_in.at[:, pl.ds(start, span)], inverse, sems.at[0]))
    pivot_copy = pltpu.make_async_copy(pivots_in.at[:, pl.ds(start, groups)], pivots, sems.at[1])
    for copy in copies:
        copy.start()
    pivot_copy.start()

    for cells in (initial, middle):
        cells[0] = jnp.zeros(cells.shape[1:], jnp.float32)
        cells[layers + 1] = jnp.zeros(cells.shape[1:], jnp.float32)
    forward[0] = jnp.zeros(forward.shape[1:], jnp.float32)
    result[layers] = jnp.zeros(result.shape[1:], jnp.float32)
    lane = lanes_of(rows)
    place = lane % SLOT
    side_noise = packed_noise[pl.ds(start, span)].reshape(rows, LANES)
    side_inverse = packed_inverse[pl.ds(start, span)].reshape(rows, LANES)
    for copy in copies:
        copy.wait()

    def first_step(layer, own):
        field = (inverse[layer] * noise[layer]).reshape(rows, columns)
        for t in range(tiles):
            initial[layer + 1, t, pl.ds(GROUP, rows), :] = field[:, t * LANES : (t + 1) * LANES]
        both = jnp.where(lane == LANES - 1, field[:, columns - LANES :], field[:, :LANES])
        return jnp.where(lane // SLOT == layer, pltpu.roll(both, layer * SLOT + 1, 1), own)

    own = lax.fori_loop(0, layers, first_step, jnp.zeros((rows, LANES), jnp.float32))

    side = jnp.where(place < 2, own, side_inverse * side_noise)
    total = jnp.where(lane >= SLOT, pltpu.roll(side, SLOT, 1), 0.0)
    total = total + jnp.where(lane < LANES - SLOT, pltpu.roll(side, LANES - SLOT, 1), 0.0)
    total = total + pltpu.roll(side, 1, 0) + pltpu.roll(side, rows - 1, 0)
    total = total + jnp.where(
        place == 3,
        pltpu.roll(side, 1, 1) + pltpu.roll(side, 2, 1),
        pltpu.roll(side, LANES - 1, 1) + pltpu.roll(side, 4, 1),
    )
    side_middle = side_inverse * (side_noise + total)
    side = jnp.where(place == 2, pltpu.roll(side, LANES - 2, 1), side)
    side_middle = jnp.where(place == 2, pltpu.roll(side_middle, LANES - 2, 1), side_middle)[GROUP : GROUP + kept]

    def second_step(layer, carry):
        totals = around(initial, side, layer, GROUP, rows)
        for t in range(tiles):
            part = pl.ds(t * LANES, LANES)
            field = inverse[layer, :, :, part] * (noise[layer, :, :, part] + totals[t].reshape(span, GROUP, LANES))
            middle[layer + 1, t, pl.ds(GROUP, rows), :] = field.reshape(rows, LANES)
        return carry

    lax.fori_loop(0, layers, second_step, 0)
    pivot_copy.wait()

    def third_step(layer, carry):
        totals = around(middle, side_middle, layer, 2 * GROUP, kept)
        inner = pl.ds(1, groups)
        for t in range(tiles):
            part = pl.ds(t * LANES, LANES)
            field = inverse[layer, inner, :, part] * (noise[layer, inner, :, part] + totals[t].reshape(groups, GROUP, LANES))
            forward[layer + 1, :, :, part] = (field + forward[layer, :, :, part]) * pivots[layer, :, :, part]
        return carry

    lax.fori_loop(0, layers, third_step, 0)

    def place_out(layer):
        return pltpu.make_async_copy(result.at[layer], out.at[layer, pl.ds(start, groups)], out_sems.at[layer])

    def last_step(step, carry):
        layer = layers - 1 - step
        result[layer] = forward[layer + 1] + pivots[layer] * result[layer + 1]
        place_out(layer).start()
        return carry

    lax.fori_loop(0, layers, last_step, 0)
    for layer in range(layers):
        place_out(layer).wait()


def window(inverse, pivots, packed_noise, packed_inverse, near, half, rest=(), partial=None):
    layers, total_groups, _, columns = pivots.shape
    is_far = partial is not None
    groups = total_groups // 2 + (1 if is_far else -1)
    span = groups + 2
    tiles = columns // LANES
    anywhere = pl.BlockSpec(memory_space=pl.ANY)
    whole = pl.BlockSpec(memory_space=pltpu.VMEM)
    operands = [inverse, pivots, packed_noise, packed_inverse, near, *rest]
    specs = [anywhere, anywhere, whole, whole, anywhere] + [anywhere] * len(rest)
    aliases = {}
    if is_far:
        aliases = {len(operands): 0}
        operands.append(partial)
        specs.append(anywhere)
    block = functools.partial(pltpu.VMEM, dtype=jnp.float32)
    padded = (layers + 2, tiles, (span + 2) * GROUP, LANES)
    return pl.pallas_call(
        functools.partial(window_kernel, half, is_far),
        in_specs=specs,
        out_specs=anywhere,
        out_shape=jax.ShapeDtypeStruct((layers, total_groups, GROUP, columns), jnp.float32),
        scratch_shapes=[
            block((layers, span, GROUP, columns)),
            block((layers, span, GROUP, columns)),
            block((layers, groups, GROUP, columns)),
            block(padded),
            block(padded),
            block((layers + 1, groups, GROUP, columns)),
            block((layers + 1, groups, GROUP, columns)),
            pltpu.SemaphoreType.DMA((4 + half,)),
            pltpu.SemaphoreType.DMA((layers,)),
        ],
        input_output_aliases=aliases,
        compiler_params=pltpu.CompilerParams(vmem_limit_bytes=32 * 1024 * 1024),
        cost_estimate=pl.CostEstimate(flops=20 * layers * kept_cells(groups, columns), bytes_accessed=16 * layers * kept_cells(groups, columns), transcendentals=0),
    )(*operands)


def kept_cells(groups, columns):
    return groups * GROUP * columns


def factors(kappa):
    pivots = []
    for layer_index in range(kappa.shape[0]):
        diagonal = 2.5 + kappa[layer_index]
        if layer_index > 0:
            diagonal = diagonal - pivots[-1]
        pivots.append(1.0 / diagonal)
    return jnp.stack(pivots, 0)


def columns_of(cells, owner, columns):
    return lax.dynamic_slice_in_dim(cells, owner * columns, columns, axis=2)


def rows_message(pairs_of_rows, corner):
    layers, two, columns = pairs_of_rows.shape
    flat = pairs_of_rows.reshape(layers * two, columns)
    corner = jnp.pad(corner, ((0, GROUP - 1), (0, columns - LANES)))
    return jnp.concatenate([flat, corner], 0)


def read_rows(message, layers, above):
    columns = message.shape[1]
    pair = message[: 2 * layers].reshape(layers, 2, columns)
    corner = message[2 * layers : 2 * layers + 1, :LANES]
    if above:
        return jnp.pad(pair, ((0, 0), (GROUP - 2, 0), (0, 0))), jnp.pad(corner, ((GROUP - 1, 0), (0, 0)))
    return jnp.pad(pair, ((0, 0), (0, GROUP - 2), (0, 0))), jnp.pad(corner, ((0, GROUP - 1), (0, 0)))


def fold(packed, columns):
    rows = packed.shape[-2]
    both = packed * four_lanes()
    both = both[..., : rows // 2, :] + jnp.roll(both[..., rows // 2 :, :], 4, axis=-1)
    wide = columns // LANES
    count = rows // 2 // GROUP
    parts = [both[..., i * GROUP : (i + 1) * GROUP, :] for i in range(count)]
    while len(parts) % wide:
        parts.append(jnp.zeros_like(parts[0]))
    lines = [jnp.concatenate(parts[i : i + wide], -1) for i in range(0, len(parts), wide)]
    return jnp.concatenate(lines, -2)


def unfold(message, rows):
    wide = message.shape[-1] // LANES
    lines = []
    for i in range(rows // 2 // GROUP):
        line, part = divmod(i, wide)
        lines.append(message[line * GROUP : (line + 1) * GROUP, part * LANES : (part + 1) * LANES])
    both = jnp.concatenate(lines, 0)
    return jnp.concatenate([both, jnp.roll(both, -4, axis=-1)], 0)


def four_lanes():
    place = jnp.arange(LANES) % SLOT
    return ((place >= 2) & (place < 6)).astype(jnp.float32)


def body(noise, kappa, mask):
    layers, rows, width = noise.shape
    count = lax.axis_size("ay")
    across = lax.axis_size("ax")
    half = count // 2
    columns = width // count
    height = rows * count
    depth = rows // GROUP
    me = lax.axis_index("ay")
    upper = me // half
    left_two = jnp.arange(LANES) % SLOT < 4

    def swap(cells, step):
        return lax.ppermute(cells, "ay", [(i, i ^ step) for i in range(count)])

    far = []
    token = me
    for step in range(count - 1, half - 1, -1):
        piece = columns_of(noise, token ^ step, columns)
        piece, token = lax.optimization_barrier((piece, token))
        far.append(swap(piece, step).reshape(layers, depth, GROUP, columns))

    inverse = mask[None].astype(jnp.float32) / (6.0 + kappa)
    packed = pack(inverse, columns, rows)[0]
    from_left = lax.ppermute(packed, "ay", [(i, i + 1) for i in range(count - 1)])
    from_right = lax.ppermute(packed, "ay", [(i + 1, i) for i in range(count - 1)])
    sides = jnp.where(left_two, from_left, from_right)
    down = rows_message(inverse[:, -2:], sides[-1:])
    up = rows_message(inverse[:, :2], sides[:1])
    from_above = lax.ppermute(down, "ax", [(i, i + 1) for i in range(across - 1)])
    from_below = lax.ppermute(up, "ax", [(i + 1, i) for i in range(across - 1)])
    above, corner_above = read_rows(from_above, layers, True)
    below, corner_below = read_rows(from_below, layers, False)
    inverse = jnp.concatenate([above, inverse, below], 1).reshape(layers, -1, GROUP, columns)
    packed_inverse = jnp.concatenate([corner_above, sides, corner_below], 0).reshape(-1, GROUP, LANES)
    pivots = factors(kappa).reshape(layers, -1, GROUP, columns)

    blocks = pack(noise, columns, rows)
    nothing = jnp.zeros_like(blocks[:1])
    sides = jnp.where(left_two, jnp.concatenate([nothing, blocks[:-1]]), jnp.concatenate([blocks[1:], nothing]))
    folded = fold(sides, columns)

    outer = lax.dynamic_slice_in_dim(noise, jnp.where(me == 0, 0, rows - 2), 2, axis=1)
    corner = lax.dynamic_slice_in_dim(sides, jnp.where(me == 0, 0, rows - 1), 1, axis=1)
    messages = jnp.stack([rows_message(outer[:, :, d * columns : (d + 1) * columns], corner[d]) for d in range(count)])
    pairs_same, pairs_other = [], []
    last = count - 1
    for i in range(across - 1):
        pairs_same += [(i * count + last, (i + 1) * count + last), ((i + 1) * count, i * count)]
        pairs_other += [(i * count + last, (i + 1) * count + half - 1), ((i + 1) * count, i * count + half)]
    own_half = lax.dynamic_slice_in_dim(messages, upper * half, half, axis=0)
    other_half = lax.dynamic_slice_in_dim(messages, (1 - upper) * half, half, axis=0)
    ends = lax.ppermute(own_half, ("ax", "ay"), pairs_same) + lax.ppermute(other_half, ("ax", "ay"), pairs_other)

    relayed = swap(lax.dynamic_slice_in_dim(folded, (1 - upper) * half, half, axis=0), half)
    direct = lax.dynamic_slice_in_dim(folded, upper * half, half, axis=0)
    extras = jnp.concatenate([direct, relayed, ends], 1)
    lines = folded.shape[1]

    near_block = jnp.zeros((layers, height // 2 + GROUP, columns), jnp.float32)
    packed_noise = jnp.zeros((height + 2 * GROUP, LANES), jnp.float32)
    extra_of = []
    for step in range(half):
        partner = me ^ step
        piece = columns_of(noise, partner, columns)
        extra = lax.dynamic_index_in_dim(extras, partner % half, 0, keepdims=False)
        if step:
            message = jnp.concatenate([piece.reshape(layers * rows, columns), extra], 0)
            message = swap(message, step)
            piece, extra = message[: layers * rows].reshape(layers, rows, columns), message[layers * rows :]
        at = (partner % half) * rows + GROUP * (1 - upper)
        near_block = lax.dynamic_update_slice_in_dim(near_block, piece, at, axis=1)
        packed_noise = lax.dynamic_update_slice_in_dim(packed_noise, unfold(extra[:lines], rows), GROUP + partner * rows, axis=0)
        packed_noise = lax.dynamic_update_slice_in_dim(
            packed_noise, unfold(extra[lines : 2 * lines], rows), GROUP + (partner ^ half) * rows, axis=0
        )
        extra_of.append(extra[2 * lines :])
    extra_of = jnp.stack(extra_of)
    top = lax.dynamic_index_in_dim(extra_of, (me % half) ^ (half - 1), 0, keepdims=False)
    bottom = lax.dynamic_index_in_dim(extra_of, me % half, 0, keepdims=False)
    above, corner_above = read_rows(top, layers, True)
    below, corner_below = read_rows(bottom, layers, False)
    packed_noise = lax.dynamic_update_slice_in_dim(packed_noise, corner_above, 0, axis=0)
    packed_noise = lax.dynamic_update_slice_in_dim(packed_noise, corner_below, GROUP + height, axis=0)
    packed_noise = packed_noise.reshape(-1, GROUP, LANES)
    near_block = lax.dynamic_update_slice_in_dim(near_block, jnp.where(upper == 0, above, below), upper * (height // 2), axis=1)
    near_block = near_block.reshape(layers, -1, GROUP, columns)
    inner = lax.dynamic_slice_in_dim(near_block, (1 - upper) * (near_block.shape[1] - 2), 2, axis=1)
    end = jnp.where(upper == 0, below, above).reshape(layers, 1, GROUP, columns)

    partial = window(inverse, pivots, packed_noise, packed_inverse, near_block, half)
    sample = window(inverse, pivots, packed_noise, packed_inverse, inner, half, (end, *far), partial)
    return sample.reshape(layers, height, columns)


def solution(mesh):
    in_specs = (P(None, ("ax", "ay"), None), P(None, "ax", "ay"), P("ax", "ay"))
    out_specs = P(None, "ax", "ay")
    return jax.shard_map(body, mesh=mesh, in_specs=in_specs, out_specs=out_specs, check_vma=False)
```

```python
import functools

import jax
import jax.numpy as jnp
from jax import lax
from jax.experimental import pallas as pl
from jax.experimental.pallas import tpu as pltpu
from jax.sharding import PartitionSpec as P

LANES = 128
SLOT = 8
GROUP = 8
MIB = 1024 * 1024

ANYWHERE = pl.BlockSpec(memory_space=pl.ANY)
WHOLE = pl.BlockSpec(memory_space=pltpu.VMEM)


def f32(*shape):
    return jax.ShapeDtypeStruct(shape, jnp.float32)


def lanes_of(rows):
    return lax.broadcasted_iota(jnp.int32, (rows, LANES), 1)


def packed_layer(first, last, layer):
    both = jnp.where(lanes_of(first.shape[0]) < LANES // 2, first, last)
    return pltpu.roll(both, (layer * SLOT + 4) % LANES, 1)


def sides_of(first, last, target, count):
    layers, depth, _, _ = first.shape
    rows = depth * GROUP
    lane = lanes_of(rows)
    place = lane % SLOT
    kept = ((place == 2) | (place == 3)) & (target > 0) | ((place == 4) | (place == 5)) & (target < count - 1)
    total = jnp.zeros((rows, LANES), jnp.float32)
    for layer in range(layers):
        turned = packed_layer(first[layer].reshape(rows, LANES), last[layer].reshape(rows, LANES), layer)
        total = jnp.where((lane // SLOT == layer) & kept, turned, total)
    return total


def fold_into(thin, packed):
    rows = packed.shape[0]
    wide = thin.shape[2] // LANES
    both = packed[: rows // 2] + pltpu.roll(packed[rows // 2 :], 4, 1)
    thin[...] = jnp.zeros(thin.shape, jnp.float32)
    for i in range(rows // 2 // GROUP):
        thin[i // wide, :, i % wide * LANES : (i % wide + 1) * LANES] = both[i * GROUP : (i + 1) * GROUP]


def unfold_into(packed, first, thin, rows):
    wide = thin.shape[2] // LANES
    for i in range(rows // 2 // GROUP):
        both = thin[i // wide, :, i % wide * LANES : (i % wide + 1) * LANES]
        packed[pl.ds(pl.multiple_of(first + i * GROUP, GROUP), GROUP), :] = both
        packed[pl.ds(pl.multiple_of(first + rows // 2 + i * GROUP, GROUP), GROUP), :] = pltpu.roll(both, LANES - 4, 1)


def strip_of(message, layers, depth):
    return message.at[pl.ds(0, layers * depth)].reshape(layers, depth, GROUP, message.shape[2])


def message_kernel(parts, tips, count, noise, *refs):
    outs = refs[: len(parts)]
    left, right, thin, rows_of, sems = refs[-5:]
    layers, depth, _, width = noise.shape
    columns = width // count
    me = lax.axis_index("ay")
    sided = [(s, part[0]) for s, part in enumerate(parts) if part[3]]
    copies = []
    for i, (s, step) in enumerate(sided):
        target = me ^ step
        at_left = pl.multiple_of(jnp.maximum(target, 1) * columns - LANES, LANES)
        at_right = pl.multiple_of(jnp.minimum(target + 1, count - 1) * columns, LANES)
        copies.append(
            [
                pltpu.make_async_copy(noise.at[:, :, :, pl.ds(at_left, LANES)], left.at[i], sems.at[0, s]),
                pltpu.make_async_copy(noise.at[:, :, :, pl.ds(at_right, LANES)], right.at[i], sems.at[1, s]),
            ]
        )
    for pair in copies:
        for copy in pair:
            copy.start()
    ends = []
    is_first = me == 0
    for i, step in enumerate(tips):
        at = pl.multiple_of((me ^ step) * columns, LANES)
        group = noise.at[:, jnp.where(is_first, 0, depth - 1), :, pl.ds(at, columns)]
        ends.append(pltpu.make_async_copy(group, rows_of.at[i], sems.at[4, i]))
        ends[-1].start()
    tip_copies = ends[:]
    ends = []
    for s, (step, lower, size, _) in enumerate(parts):
        at = pl.multiple_of((me ^ step) * columns, LANES)
        if size:
            piece = noise.at[pl.ds(lower, size), :, :, pl.ds(at, columns)]
            ends.append(pltpu.make_async_copy(piece, strip_of(outs[s], size, depth), sems.at[2, s]))
            ends[-1].start()
    for i, (s, step) in enumerate(sided):
        for copy in copies[i]:
            copy.wait()
        sides = sides_of(right.at[i], left.at[i], me ^ step, count)
        fold_into(thin.at[i], sides)
        if step in tips:
            at = tips.index(step)
            tip_copies[at].wait()
            tip = refs[len(parts)]
            base = at * (2 * layers + GROUP)
            for layer in range(layers):
                group = rows_of[at, layer]
                tip[base + 2 * layer : base + 2 * layer + 2, :] = jnp.where(is_first, group[:2], group[GROUP - 2 :])
            end = base + 2 * layers
            tip[end : end + GROUP, :] = jnp.zeros((GROUP, columns), jnp.float32)
            tip[end : end + 1, :LANES] = jnp.where(is_first, sides[:1], sides[-1:])
        to = outs[s].at[pl.ds(parts[s][2] * depth, thin.shape[1])]
        ends.append(pltpu.make_async_copy(thin.at[i], to, sems.at[3, s]))
        ends[-1].start()
    for end in ends:
        end.wait()


def messages(noise, parts, count, tips=()):
    layers, depth, _, width = noise.shape
    columns = width // count
    lines = -(-depth // 2 // (columns // LANES))
    shapes = [f32(part[2] * depth + (lines if part[3] else 0), GROUP, columns) for part in parts]
    block = functools.partial(pltpu.VMEM, dtype=jnp.float32)
    sided = sum(part[3] for part in parts)
    shapes += [f32(len(tips) * (2 * layers + GROUP), columns)] if tips else []
    tile = (sided, layers, depth, GROUP, LANES)
    return pl.pallas_call(
        functools.partial(message_kernel, parts, tips, count),
        in_specs=[ANYWHERE],
        out_specs=[ANYWHERE] * len(parts) + [WHOLE] * (len(shapes) - len(parts)),
        out_shape=shapes,
        scratch_shapes=[
            block(tile),
            block(tile),
            block((sided, lines, GROUP, columns)),
            block((max(1, len(tips)), layers, GROUP, columns)),
            pltpu.SemaphoreType.DMA((5, max(len(parts), len(tips)))),
        ],
        compiler_params=pltpu.CompilerParams(vmem_limit_bytes=16 * MIB),
    )(noise)


def factor_kernel(kappa, mask, inverse, pivots, packed):
    layers, rows, columns = kappa.shape
    lane = lanes_of(rows)
    active = mask[...].astype(jnp.float32)
    total = jnp.zeros((rows, LANES), jnp.float32)
    pivot = jnp.zeros((rows, columns), jnp.float32)
    for layer in range(layers):
        value = kappa[layer]
        scale = active / (6.0 + value)
        inverse[layer] = scale
        pivot = 1.0 / (2.5 + value - pivot)
        pivots[layer] = pivot
        turned = packed_layer(scale[:, :LANES], scale[:, columns - LANES :], layer)
        total = jnp.where(lane // SLOT == layer, turned, total)
    packed[...] = total


def coefficients(kappa, mask, rows=32):
    layers, height, columns = kappa.shape
    block = pl.BlockSpec((layers, rows, columns), lambda r: (0, r, 0))
    return pl.pallas_call(
        factor_kernel,
        grid=(height // rows,),
        in_specs=[block, pl.BlockSpec((rows, columns), lambda r: (r, 0))],
        out_specs=[block, block, pl.BlockSpec((rows, LANES), lambda r: (r, 0))],
        out_shape=[f32(*kappa.shape), f32(*kappa.shape), f32(height, LANES)],
        compiler_params=pltpu.CompilerParams(vmem_limit_bytes=16 * MIB),
    )(kappa, mask)


def chunks(groups, size=4):
    return [(first, min(size, groups - first)) for first in range(0, groups, size)]


def around(cells, sides, layer, first, rows):
    tiles = cells.shape[1]
    lane = lanes_of(rows)
    side = pltpu.roll(sides[pl.ds(first - GROUP, rows), :], LANES - 3 - layer * SLOT, 1)
    centre = [cells[layer + 1, t, pl.ds(first, rows), :] for t in range(tiles)]
    left = [pltpu.roll(x, 1, 1) for x in centre]
    right = [pltpu.roll(x, LANES - 1, 1) for x in centre]
    totals = []
    for t in range(tiles):
        total = cells[layer + 1, t, pl.ds(first + 1, rows), :] + cells[layer + 1, t, pl.ds(first - 1, rows), :]
        total = total + jnp.where(lane == 0, side if t == 0 else left[t - 1], left[t])
        total = total + jnp.where(lane == LANES - 1, side if t == tiles - 1 else right[t + 1], right[t])
        totals.append(total + cells[layer, t, pl.ds(first, rows), :] + cells[layer + 2, t, pl.ds(first, rows), :])
    return totals


def solve(noise, inverse, pivots, base, packed_noise, packed_inverse, initial, middle, forward, packed, wait_pivots, finished, unroll=1):
    layers, columns = noise.shape[0], noise.shape[3]
    groups = forward.shape[1]
    span = groups + 2
    rows = span * GROUP
    tiles = columns // LANES
    own, sides, sides_middle = packed
    for cells in (initial, middle):
        cells[0] = jnp.zeros(cells.shape[1:], jnp.float32)
        cells[layers + 1] = jnp.zeros(cells.shape[1:], jnp.float32)
    forward[0] = jnp.zeros(forward.shape[1:], jnp.float32)
    forward[layers + 1] = jnp.zeros(forward.shape[1:], jnp.float32)
    own[...] = jnp.zeros(own.shape, jnp.float32)

    def first_step(layer, carry):
        for first, size in chunks(span):
            height = size * GROUP
            lane = lanes_of(height)
            at = pl.ds(base + first, size)
            field = (inverse[layer, at] * noise[layer, at]).reshape(height, columns)
            for t in range(tiles):
                initial[layer + 1, t, pl.ds((first + 1) * GROUP, height), :] = field[:, t * LANES : (t + 1) * LANES]
            both = jnp.where(lane == LANES - 1, field[:, columns - LANES :], field[:, :LANES])
            turned = pltpu.roll(both, layer * SLOT + 1, 1)
            here = pl.ds(first * GROUP, height)
            own[here, :] = jnp.where(lane // SLOT == layer, turned, own[here, :])
        return carry

    lax.fori_loop(0, layers, first_step, 0, unroll=unroll)

    lane = lanes_of(rows)
    place = lane % SLOT
    side = jnp.where(place < 2, own[...], packed_inverse * packed_noise)
    total = jnp.where(lane >= SLOT, pltpu.roll(side, SLOT, 1), 0.0)
    total = total + jnp.where(lane < LANES - SLOT, pltpu.roll(side, LANES - SLOT, 1), 0.0)
    total = total + pltpu.roll(side, 1, 0) + pltpu.roll(side, rows - 1, 0)
    total = total + jnp.where(
        place == 3,
        pltpu.roll(side, 1, 1) + pltpu.roll(side, 2, 1),
        pltpu.roll(side, LANES - 1, 1) + pltpu.roll(side, 4, 1),
    )
    side_middle = packed_inverse * (packed_noise + total)
    sides[...] = jnp.where(place == 2, pltpu.roll(side, LANES - 2, 1), side)
    sides_middle[...] = jnp.where(place == 2, pltpu.roll(side_middle, LANES - 2, 1), side_middle)

    def second_step(layer, carry):
        for first, size in chunks(span):
            height = size * GROUP
            at = pl.ds(base + first, size)
            totals = around(initial, sides, layer, (first + 1) * GROUP, height)
            for t in range(tiles):
                part = pl.ds(t * LANES, LANES)
                field = inverse[layer, at, :, part] * (noise[layer, at, :, part] + totals[t].reshape(size, GROUP, LANES))
                middle[layer + 1, t, pl.ds((first + 1) * GROUP, height), :] = field.reshape(height, LANES)
        return carry

    lax.fori_loop(0, layers, second_step, 0, unroll=unroll)
    wait_pivots()

    def third_step(layer, carry):
        for first, size in chunks(groups):
            height = size * GROUP
            at = pl.ds(base + 1 + first, size)
            here = pl.ds(first, size)
            totals = around(middle, sides_middle, layer, (first + 2) * GROUP, height)
            for t in range(tiles):
                part = pl.ds(t * LANES, LANES)
                field = inverse[layer, at, :, part] * (noise[layer, at, :, part] + totals[t].reshape(size, GROUP, LANES))
                pivot = pivots[layer, pl.ds(base + first, size), :, part]
                forward[layer + 1, here, :, part] = (field + forward[layer, here, :, part]) * pivot
        return carry

    lax.fori_loop(0, layers, third_step, 0, unroll=unroll)

    def last_step(step, carry):
        layer = layers - 1 - step
        for first, size in chunks(groups):
            here = pl.ds(first, size)
            pivot = pivots[layer, pl.ds(base + first, size)]
            forward[layer + 1, here] = forward[layer + 1, here] + pivot * forward[layer + 2, here]
        finished(layer)
        return carry

    lax.fori_loop(0, layers, last_step, 0, unroll=unroll)


def solve_scratch(layers, groups, columns):
    block = functools.partial(pltpu.VMEM, dtype=jnp.float32)
    padded = (layers + 2, columns // LANES, (groups + 4) * GROUP, LANES)
    rows = (groups + 2) * GROUP
    return [
        block(padded),
        block(padded),
        block((layers + 2, groups, GROUP, columns)),
        block((rows, LANES)),
        block((rows, LANES)),
        block((rows, LANES)),
    ]


def merged_sides(paired, other):
    odd = lax.axis_index("ay") % 2
    is_left = (lanes_of(paired.shape[0]) % SLOT < 4).astype(jnp.int32)
    return jnp.where(is_left == odd, paired, other)


def last_two(half):
    me = lax.axis_index("ay")
    one, other = me ^ half, me ^ (half + 1)
    return jnp.minimum(one, other), one, other


def block_kernel(half, depth, *refs):
    known = 2 * half - 3
    inverse_in, pivots_in, own_piece, own_sides = refs[:4]
    pieces = refs[4 : 4 + known]
    paired, other, above, below = refs[4 + known : 8 + known]
    out, noise_out, inverse_out, pivots_out, packed_noise, packed_inverse = refs[8 + known : 14 + known]
    noise, inverse, pivots, thin, *scratch, sems, out_sems = refs[14 + known :]
    initial, middle, forward, own, sides, sides_middle = scratch
    layers, groups, _, columns = pivots_in.shape
    rows, height, lines = depth * GROUP, groups * GROUP, thin.shape[1]
    me = lax.axis_index("ay")
    last = last_two(half)[0] * depth
    steps = [0] + [step for step in range(2 * half - 1, 0, -1) if step not in (half, half + 1)]

    inverse_copy = pltpu.make_async_copy(inverse_in, inverse.at[:, pl.ds(2, groups)], sems.at[0])
    pivot_copy = pltpu.make_async_copy(pivots_in, pivots.at[:, pl.ds(1, groups)], sems.at[1])
    waits, thin_copies = [inverse_copy], []
    inverse_copy.start()
    for index, step in enumerate(steps):
        target = noise.at[:, pl.ds(2 + (me ^ step) * depth, depth)]
        if step:
            message = pieces[index - 1]
            piece = strip_of(message, layers, depth)
            side = message.at[pl.ds(layers * depth, lines)]
        else:
            piece = own_piece.at[:, :, :, pl.ds(pl.multiple_of(me * columns, LANES), columns)]
            side = own_sides
        waits.append(pltpu.make_async_copy(piece, target, sems.at[2 + index]))
        waits[-1].start()
        thin_copies.append(pltpu.make_async_copy(side, thin.at[index], sems.at[2 + len(steps) + index]))
        thin_copies[-1].start()
    pivot_copy.start()

    nothing = jnp.zeros((layers, GROUP, columns), jnp.float32)
    for ref in (noise, inverse):
        for group in (0, 1, groups + 2, groups + 3):
            ref[:, group] = nothing
    pivots[:, 0] = nothing
    pivots[:, groups + 1] = nothing
    packed_noise[...] = jnp.zeros(packed_noise.shape, jnp.float32)
    packed_inverse[...] = jnp.zeros(packed_inverse.shape, jnp.float32)
    packed_inverse[2 * GROUP : 2 * GROUP + height] = merged_sides(paired[...], other[...])
    end = 4 * layers
    for message, group, place, row in ((above, 1, GROUP - 2, 2 * GROUP - 1), (below, groups + 2, 0, 2 * GROUP + height)):
        for layer in range(layers):
            noise[layer, group, place : place + 2, :] = message[2 * layer : 2 * layer + 2, :]
            inverse[layer, group, place : place + 2, :] = message[2 * (layers + layer) : 2 * (layers + layer) + 2, :]
        packed_noise[row : row + 1] = message[end : end + 1, :LANES]
        packed_inverse[row : row + 1] = message[end : end + 1, LANES : 2 * LANES]
    for index, step in enumerate(steps):
        thin_copies[index].wait()
        unfold_into(packed_noise, 2 * GROUP + (me ^ step) * rows, thin.at[index], rows)
    for copy in waits:
        copy.wait()
    windows = [
        pltpu.make_async_copy(noise.at[:, pl.ds(last, 2)], noise_out.at[:, pl.ds(0, 2)], sems.at[0]),
        pltpu.make_async_copy(noise.at[:, pl.ds(last + 2 * depth + 2, 2)], noise_out.at[:, pl.ds(2, 2)], sems.at[2]),
        pltpu.make_async_copy(inverse.at[:, pl.ds(last, 2 * depth + 4)], inverse_out, sems.at[3]),
    ]
    for copy in windows:
        copy.start()
    pivot_window = pltpu.make_async_copy(pivots.at[:, pl.ds(last, 2 * depth + 2)], pivots_out, sems.at[6])

    def wait_pivots():
        pivot_copy.wait()
        pivot_window.start()

    def place_out(layer):
        return pltpu.make_async_copy(forward.at[layer + 1], out.at[layer], out_sems.at[layer])

    inner = pl.ds(GROUP, height + 2 * GROUP)
    solve(
        noise, inverse, pivots, 1, packed_noise[inner, :], packed_inverse[inner, :],
        initial, middle, forward, (own, sides, sides_middle), wait_pivots, lambda layer: place_out(layer).start(),
    )
    for layer in range(layers):
        place_out(layer).wait()
    for copy in windows:
        copy.wait()
    pivot_window.wait()


def solve_block(inverse, pivots, own_piece, own_sides, pieces, paired, other, above, below, half, depth):
    layers, groups, _, columns = pivots.shape
    block = functools.partial(pltpu.VMEM, dtype=jnp.float32)
    packed = f32((groups + 4) * GROUP, LANES)
    return pl.pallas_call(
        functools.partial(block_kernel, half, depth),
        in_specs=[ANYWHERE] * (4 + len(pieces)) + [WHOLE] * 4,
        out_specs=[ANYWHERE] * 4 + [WHOLE] * 2,
        out_shape=[
            f32(layers, groups, GROUP, columns),
            f32(layers, 4, GROUP, columns),
            f32(layers, 2 * depth + 4, GROUP, columns),
            f32(layers, 2 * depth + 2, GROUP, columns),
            packed,
            packed,
        ],
        scratch_shapes=[
            block((layers, groups + 4, GROUP, columns)),
            block((layers, groups + 4, GROUP, columns)),
            block((layers, groups + 2, GROUP, columns)),
            block((len(pieces) + 1, *own_sides.shape)),
            *solve_scratch(layers, groups, columns),
            pltpu.SemaphoreType.DMA((2 * len(pieces) + 7,)),
            pltpu.SemaphoreType.DMA((layers,)),
        ],
        compiler_params=pltpu.CompilerParams(vmem_limit_bytes=40 * MIB),
    )(inverse, pivots, own_piece, own_sides, *pieces, paired, other, above, below)


def edge_kernel(steps, count, own_piece, own_sides, inverse, paired, other, *refs):
    pieces, tips = refs[: len(steps) - 1], refs[len(steps) - 1 : len(steps) + 1]
    up, down, ends, thin, outer, sems = refs[len(steps) + 1 :]
    layers, columns = ends.shape[1], ends.shape[3]
    depth, lines = own_piece.shape[1], thin.shape[1]
    height = paired.shape[0]
    half = count // 2
    wide = columns // LANES
    me = lax.axis_index("ay")
    copies = [
        pltpu.make_async_copy(inverse.at[:, 0], outer.at[0], sems.at[0]),
        pltpu.make_async_copy(inverse.at[:, inverse.shape[1] - 1], outer.at[1], sems.at[1]),
    ]
    for copy in copies:
        copy.start()

    def fetch(step, piece, side):
        if step:
            rows, sides = strip_of(piece, layers, depth), piece.at[pl.ds(layers * depth, lines)]
        else:
            rows, sides = own_piece.at[:, :, :, pl.ds(pl.multiple_of(me * columns, LANES), columns)], own_sides
        pltpu.make_async_copy(rows.at[:, side * (depth - 1)], ends.at[side], sems.at[2 + side]).start()
        pltpu.make_async_copy(sides, thin.at[side], sems.at[4 + side]).start()

    for step, piece in zip(steps, (None, *pieces)):
        for side in range(2):
            pl.when((me ^ step) == side * (count - 1))(functools.partial(fetch, step, piece, side))
    for copy in copies:
        copy.wait()
    for side, (out, place, row) in enumerate(((up, 0, 0), (down, GROUP - 2, height - 1))):
        target = side * (count - 1)
        late = ((me ^ half) == target) | ((me ^ (half + 1)) == target)

        def wait(side):
            pltpu.make_async_copy(ends.at[side], ends.at[side], sems.at[2 + side]).wait()
            pltpu.make_async_copy(thin.at[side], thin.at[side], sems.at[4 + side]).wait()

        pl.when(jnp.logical_not(late))(functools.partial(wait, side))
        tip = jnp.where((me ^ half) == target, tips[0][: 2 * layers + GROUP], tips[1][...])
        for layer in range(layers):
            out[2 * layer : 2 * layer + 2, :] = jnp.where(
                late, tip[2 * layer : 2 * layer + 2, :], ends[side, layer, place : place + 2, :]
            )
            out[2 * (layers + layer) : 2 * (layers + layer) + 2, :] = outer[side, layer, place : place + 2, :]
        if side:
            i = depth // 2 - 1
            both = thin[side, i // wide, :, i % wide * LANES : (i % wide + 1) * LANES]
            corner = pltpu.roll(both, LANES - 4, 1)[GROUP - 1 :]
        else:
            corner = thin[side, 0, 0:1, :LANES]
        end = 4 * layers
        out[end : end + GROUP, :] = jnp.zeros((GROUP, columns), jnp.float32)
        out[end : end + 1, :LANES] = jnp.where(late, tip[2 * layers : 2 * layers + 1, :LANES], corner)
        out[end : end + 1, LANES : 2 * LANES] = merged_sides(paired[row : row + 1, :], other[row : row + 1, :])


def edges(own_piece, own_sides, inverse, paired, other, steps, pieces, tips, count):
    layers, _, _, columns = inverse.shape
    outer = f32(4 * layers + GROUP, columns)
    block = functools.partial(pltpu.VMEM, dtype=jnp.float32)
    return pl.pallas_call(
        functools.partial(edge_kernel, steps, count),
        in_specs=[ANYWHERE] * 3 + [WHOLE] * 2 + [ANYWHERE] * len(pieces) + [WHOLE] * 2,
        out_specs=[WHOLE] * 2,
        out_shape=[outer, outer],
        scratch_shapes=[
            block((2, layers, GROUP, columns)),
            block((2, *own_sides.shape)),
            block((2, layers, GROUP, columns)),
            pltpu.SemaphoreType.DMA((6,)),
        ],
        compiler_params=pltpu.CompilerParams(vmem_limit_bytes=12 * MIB),
    )(own_piece, own_sides, inverse, paired, other, *pieces, *tips)


def tail_kernel(half, depth, known, inverse_in, pivots_in, packed_noise, packed_inverse, before, lower, upper, partial, out, noise, inverse, pivots, packed, thin, *rest):
    del partial
    initial, middle, forward, own, sides, sides_middle, sems, out_sems = rest
    layers, groups, _, columns = pivots.shape
    count = 2 * half
    last, one, other = last_two(half)
    part = lower.shape[0] // depth
    lines = thin.shape[1]
    at_one, at_other = (pl.ds(2 + (strip - last) * depth, depth) for strip in (one, other))
    copies = [
        pltpu.make_async_copy(strip_of(upper, layers - part, depth), noise.at[pl.ds(part, layers - part), at_one], sems.at[0]),
        pltpu.make_async_copy(strip_of(lower, part, depth), noise.at[pl.ds(0, part), at_one], sems.at[1]),
        pltpu.make_async_copy(strip_of(before, layers, depth), noise.at[:, at_other], sems.at[2]),
        pltpu.make_async_copy(known.at[:, pl.ds(0, 2)], noise.at[:, pl.ds(0, 2)], sems.at[3]),
        pltpu.make_async_copy(known.at[:, pl.ds(2, 2)], noise.at[:, pl.ds(2 * depth + 2, 2)], sems.at[4]),
        pltpu.make_async_copy(inverse_in, inverse, sems.at[6]),
        pltpu.make_async_copy(upper.at[pl.ds((layers - part) * depth, lines)], thin.at[0], sems.at[7]),
        pltpu.make_async_copy(before.at[pl.ds(layers * depth, lines)], thin.at[1], sems.at[8]),
    ]
    pivot_copy = pltpu.make_async_copy(pivots_in, pivots, sems.at[5])
    for copy in (*copies, pivot_copy):
        copy.start()
    inner = pl.ds(pl.multiple_of(last * depth * GROUP, GROUP), (groups + 2) * GROUP)
    packed[...] = packed_noise[inner, :]
    for copy in copies:
        copy.wait()
    for index, strip in enumerate((one, other)):
        unfold_into(packed, (2 + (strip - last) * depth) * GROUP, thin.at[index], depth * GROUP)

    def place_out(layer):
        return pltpu.make_async_copy(
            forward.at[layer + 1, pl.ds(1, 2 * depth)], out.at[layer, pl.ds(last * depth, 2 * depth)], out_sems.at[layer]
        )

    solve(
        noise, inverse, pivots, 0, packed[...], packed_inverse[inner, :],
        initial, middle, forward, (own, sides, sides_middle), pivot_copy.wait, lambda layer: place_out(layer).start(), layers,
    )

    def edge(own_group, to, sem):
        return pltpu.make_async_copy(forward.at[pl.ds(1, layers), pl.ds(own_group, 1)], out.at[:, pl.ds(to, 1)], sem)

    above = edge(0, jnp.maximum(last * depth - 1, 0), sems.at[0])
    below = edge(groups - 1, jnp.minimum((last + 2) * depth, count * depth - 1), sems.at[1])
    pl.when(last > 0)(above.start)
    pl.when(last < count - 2)(below.start)
    for layer in range(layers):
        place_out(layer).wait()
    pl.when(last > 0)(above.wait)
    pl.when(last < count - 2)(below.wait)


def solve_tail(sides, inverse, pivots, packed_noise, packed_inverse, before, lower, upper, partial, half, depth):
    layers, groups, _, columns = pivots.shape
    block = functools.partial(pltpu.VMEM, dtype=jnp.float32)
    return pl.pallas_call(
        functools.partial(tail_kernel, half, depth),
        in_specs=[ANYWHERE] * 3 + [WHOLE] * 2 + [ANYWHERE] * 4,
        out_specs=ANYWHERE,
        out_shape=f32(*partial.shape),
        scratch_shapes=[
            block((layers, groups + 2, GROUP, columns)),
            block((layers, groups + 2, GROUP, columns)),
            block((layers, groups, GROUP, columns)),
            block(((groups + 2) * GROUP, LANES)),
            block((2, before.shape[0] - layers * depth, GROUP, columns)),
            *solve_scratch(layers, groups, columns),
            pltpu.SemaphoreType.DMA((9,)),
            pltpu.SemaphoreType.DMA((layers,)),
        ],
        input_output_aliases={8: 0},
        compiler_params=pltpu.CompilerParams(vmem_limit_bytes=20 * MIB),
    )(sides, inverse, pivots, packed_noise, packed_inverse, before, lower, upper, partial)


def after(cells, *tokens):
    return lax.optimization_barrier((cells, *tokens))[0]


def body(noise, kappa, mask):
    layers, rows, width = noise.shape
    count = lax.axis_size("ay")
    across = lax.axis_size("ax")
    half = count // 2
    depth = rows // GROUP

    def swap(cells, step):
        return lax.ppermute(cells, "ay", [(i, i ^ step) for i in range(count)])

    def grouped(cells):
        return cells.reshape(layers, -1, GROUP, cells.shape[2])

    noise = grouped(noise)
    part = layers // 2
    first, own, split = count - 1, 0, half
    specs = {first: (first, 0, layers, True)}
    for step in [*range(count - 2, half, -1), *range(half - 1, 0, -1)]:
        specs[step] = (step, 0, layers, True)
    specs["lower"], specs["upper"] = (split, 0, part, False), (split, part, layers - part, True)
    specs[own] = (own, 0, 0, True)
    parts = {first: messages(noise, (specs.pop(first),), count)[0]}
    late = (half, half + 1)
    *made, tip = messages(after(noise, parts[first]), tuple(specs.values()), count, late)
    parts.update(zip(specs, made))
    inverse, pivots, packed = coefficients(after(kappa, parts[first]), mask)

    got = {first: swap(parts[first], first)}
    between = [pair for i in range(1, count - 1, 2) for pair in ((i, i + 1), (i + 1, i))]
    tip = lax.ppermute(tip, "ay", [(0, half), (count - 1, half - 1)])
    handed = swap(tip[tip.shape[0] // 2 :], 1)
    paired = swap(packed, 1)
    other = lax.ppermute(packed, "ay", between)
    for step in range(count - 2, half + 1, -1):
        got[step] = swap(after(parts[step], paired), step)
    got[half + 1] = swap(after(parts[half + 1], other, handed), half + 1)
    for step in range(half - 1, 1, -1):
        got[step] = swap(after(parts[step], other, handed), step)
    got[1] = swap(after(parts[1], got[first]), 1)
    lower = swap(after(parts["lower"], got[half + 2]), split)
    upper = swap(after(parts["upper"], got[half + 2]), split)
    inverse, pivots = grouped(inverse), grouped(pivots)

    steps = (0, *(step for step in range(count - 1, 0, -1) if step not in late))
    up, down = edges(
        noise, parts[0], inverse, paired, other, steps, [got[step] for step in steps[1:]], (tip, handed), count
    )
    above = lax.ppermute(down, "ax", [(i, i + 1) for i in range(across - 1)])
    below = lax.ppermute(up, "ax", [(i + 1, i) for i in range(across - 1)])
    partial, noise_part, inverse_part, pivots_part, packed_noise, packed_inverse = solve_block(
        inverse, pivots, noise, parts[0], [got[step] for step in steps[1:]], paired, other, above, below, half, depth
    )
    sample = solve_tail(
        noise_part, inverse_part, pivots_part, packed_noise, packed_inverse, got[half + 1], lower, upper, partial, half, depth
    )
    return sample.reshape(layers, rows * count, -1)


def solution(mesh):
    in_specs = (P(None, ("ax", "ay"), None), P(None, "ax", "ay"), P("ax", "ay"))
    out_specs = P(None, "ax", "ay")
    return jax.shard_map(body, mesh=mesh, in_specs=in_specs, out_specs=out_specs, check_vma=False)
```

```python
import functools

import jax
import jax.numpy as jnp
from jax import lax
from jax.experimental import pallas as pl
from jax.experimental.pallas import tpu as pltpu
from jax.sharding import PartitionSpec as P

LANES = 128
SLOT = 8
GROUP = 8
MIB = 1024 * 1024

ANYWHERE = pl.BlockSpec(memory_space=pl.ANY)
WHOLE = pl.BlockSpec(memory_space=pltpu.VMEM)


def f32(*shape):
    return jax.ShapeDtypeStruct(shape, jnp.float32)


def lanes_of(rows):
    return lax.broadcasted_iota(jnp.int32, (rows, LANES), 1)


def packed_layer(first, last, layer):
    both = jnp.where(lanes_of(first.shape[0]) < LANES // 2, first, last)
    return pltpu.roll(both, (layer * SLOT + 4) % LANES, 1)


def sides_of(first, last, target, count):
    layers, depth, _, _ = first.shape
    rows = depth * GROUP
    lane = lanes_of(rows)
    place = lane % SLOT
    kept = ((place == 2) | (place == 3)) & (target > 0) | ((place == 4) | (place == 5)) & (target < count - 1)
    total = jnp.zeros((rows, LANES), jnp.float32)
    for layer in range(layers):
        turned = packed_layer(first[layer].reshape(rows, LANES), last[layer].reshape(rows, LANES), layer)
        total = jnp.where((lane // SLOT == layer) & kept, turned, total)
    return total


def fold_into(thin, packed):
    rows = packed.shape[0]
    wide = thin.shape[2] // LANES
    both = packed[: rows // 2] + pltpu.roll(packed[rows // 2 :], 4, 1)
    thin[...] = jnp.zeros(thin.shape, jnp.float32)
    for i in range(rows // 2 // GROUP):
        thin[i // wide, :, i % wide * LANES : (i % wide + 1) * LANES] = both[i * GROUP : (i + 1) * GROUP]


def unfold_into(packed, first, thin, rows):
    wide = thin.shape[2] // LANES
    for i in range(rows // 2 // GROUP):
        both = thin[i // wide, :, i % wide * LANES : (i % wide + 1) * LANES]
        packed[pl.ds(pl.multiple_of(first + i * GROUP, GROUP), GROUP), :] = both
        packed[pl.ds(pl.multiple_of(first + rows // 2 + i * GROUP, GROUP), GROUP), :] = pltpu.roll(both, LANES - 4, 1)


def strip_of(message, layers, depth):
    return message.at[pl.ds(0, layers * depth)].reshape(layers, depth, GROUP, message.shape[2])


def message_kernel(parts, tips, count, noise, *refs):
    outs = refs[: len(parts)]
    left, right, thin, rows_of, sems = refs[-5:]
    layers, depth, _, width = noise.shape
    columns = width // count
    me = lax.axis_index("ay")
    sided = [(s, part[0]) for s, part in enumerate(parts) if part[3]]
    copies = []
    for i, (s, step) in enumerate(sided):
        target = me ^ step
        at_left = pl.multiple_of(jnp.maximum(target, 1) * columns - LANES, LANES)
        at_right = pl.multiple_of(jnp.minimum(target + 1, count - 1) * columns, LANES)
        copies.append(
            [
                pltpu.make_async_copy(noise.at[:, :, :, pl.ds(at_left, LANES)], left.at[i], sems.at[0, s]),
                pltpu.make_async_copy(noise.at[:, :, :, pl.ds(at_right, LANES)], right.at[i], sems.at[1, s]),
            ]
        )
    for pair in copies:
        for copy in pair:
            copy.start()
    ends = []
    is_first = me == 0
    for i, step in enumerate(tips):
        at = pl.multiple_of((me ^ step) * columns, LANES)
        group = noise.at[:, jnp.where(is_first, 0, depth - 1), :, pl.ds(at, columns)]
        ends.append(pltpu.make_async_copy(group, rows_of.at[i], sems.at[4, i]))
        ends[-1].start()
    tip_copies = ends[:]
    ends = []
    for s, (step, lower, size, _) in enumerate(parts):
        at = pl.multiple_of((me ^ step) * columns, LANES)
        if size:
            piece = noise.at[pl.ds(lower, size), :, :, pl.ds(at, columns)]
            ends.append(pltpu.make_async_copy(piece, strip_of(outs[s], size, depth), sems.at[2, s]))
            ends[-1].start()
    for i, (s, step) in enumerate(sided):
        for copy in copies[i]:
            copy.wait()
        sides = sides_of(right.at[i], left.at[i], me ^ step, count)
        fold_into(thin.at[i], sides)
        if step in tips:
            at = tips.index(step)
            tip_copies[at].wait()
            tip = refs[len(parts)]
            base = at * (2 * layers + GROUP)
            for layer in range(layers):
                group = rows_of[at, layer]
                tip[base + 2 * layer : base + 2 * layer + 2, :] = jnp.where(is_first, group[:2], group[GROUP - 2 :])
            end = base + 2 * layers
            tip[end : end + GROUP, :] = jnp.zeros((GROUP, columns), jnp.float32)
            tip[end : end + 1, :LANES] = jnp.where(is_first, sides[:1], sides[-1:])
        to = outs[s].at[pl.ds(parts[s][2] * depth, thin.shape[1])]
        ends.append(pltpu.make_async_copy(thin.at[i], to, sems.at[3, s]))
        ends[-1].start()
    for end in ends:
        end.wait()


def messages(noise, parts, count, tips=()):
    layers, depth, _, width = noise.shape
    columns = width // count
    lines = -(-depth // 2 // (columns // LANES))
    shapes = [f32(part[2] * depth + (lines if part[3] else 0), GROUP, columns) for part in parts]
    block = functools.partial(pltpu.VMEM, dtype=jnp.float32)
    sided = sum(part[3] for part in parts)
    shapes += [f32(len(tips) * (2 * layers + GROUP), columns)] if tips else []
    tile = (sided, layers, depth, GROUP, LANES)
    return pl.pallas_call(
        functools.partial(message_kernel, parts, tips, count),
        in_specs=[ANYWHERE],
        out_specs=[ANYWHERE] * len(parts) + [WHOLE] * (len(shapes) - len(parts)),
        out_shape=shapes,
        scratch_shapes=[
            block(tile),
            block(tile),
            block((sided, lines, GROUP, columns)),
            block((max(1, len(tips)), layers, GROUP, columns)),
            pltpu.SemaphoreType.DMA((5, max(len(parts), len(tips)))),
        ],
        compiler_params=pltpu.CompilerParams(vmem_limit_bytes=16 * MIB),
    )(noise)


def factor_kernel(kappa, mask, inverse, pivots, packed):
    layers, rows, columns = kappa.shape
    lane = lanes_of(rows)
    active = mask[...].astype(jnp.float32)
    total = jnp.zeros((rows, LANES), jnp.float32)
    pivot = jnp.zeros((rows, columns), jnp.float32)
    for layer in range(layers):
        value = kappa[layer]
        scale = active / (6.0 + value)
        inverse[layer] = scale
        pivot = 1.0 / (2.5 + value - pivot)
        pivots[layer] = pivot
        turned = packed_layer(scale[:, :LANES], scale[:, columns - LANES :], layer)
        total = jnp.where(lane // SLOT == layer, turned, total)
    packed[...] = total


def coefficients(kappa, mask, rows=32):
    layers, height, columns = kappa.shape
    block = pl.BlockSpec((layers, rows, columns), lambda r: (0, r, 0))
    return pl.pallas_call(
        factor_kernel,
        grid=(height // rows,),
        in_specs=[block, pl.BlockSpec((rows, columns), lambda r: (r, 0))],
        out_specs=[block, block, pl.BlockSpec((rows, LANES), lambda r: (r, 0))],
        out_shape=[f32(*kappa.shape), f32(*kappa.shape), f32(height, LANES)],
        compiler_params=pltpu.CompilerParams(vmem_limit_bytes=16 * MIB),
    )(kappa, mask)


def chunks(groups, size=4):
    return [(first, min(size, groups - first)) for first in range(0, groups, size)]


def around(cells, sides, layer, first, rows):
    tiles = cells.shape[1]
    lane = lanes_of(rows)
    side = pltpu.roll(sides[pl.ds(first - GROUP, rows), :], LANES - 3 - layer * SLOT, 1)
    centre = [cells[layer + 1, t, pl.ds(first, rows), :] for t in range(tiles)]
    left = [pltpu.roll(x, 1, 1) for x in centre]
    right = [pltpu.roll(x, LANES - 1, 1) for x in centre]
    totals = []
    for t in range(tiles):
        total = cells[layer + 1, t, pl.ds(first + 1, rows), :] + cells[layer + 1, t, pl.ds(first - 1, rows), :]
        total = total + jnp.where(lane == 0, side if t == 0 else left[t - 1], left[t])
        total = total + jnp.where(lane == LANES - 1, side if t == tiles - 1 else right[t + 1], right[t])
        totals.append(total + cells[layer, t, pl.ds(first, rows), :] + cells[layer + 2, t, pl.ds(first, rows), :])
    return totals


def solve(noise, inverse, pivots, base, packed_noise, packed_inverse, initial, middle, forward, packed, wait_pivots, finished, unroll=1):
    layers, columns = noise.shape[0], noise.shape[3]
    groups = forward.shape[1]
    span = groups + 2
    rows = span * GROUP
    tiles = columns // LANES
    own, sides, sides_middle = packed
    for cells in (initial, middle):
        cells[0] = jnp.zeros(cells.shape[1:], jnp.float32)
        cells[layers + 1] = jnp.zeros(cells.shape[1:], jnp.float32)
    forward[0] = jnp.zeros(forward.shape[1:], jnp.float32)
    forward[layers + 1] = jnp.zeros(forward.shape[1:], jnp.float32)
    own[...] = jnp.zeros(own.shape, jnp.float32)

    def first_step(layer, carry):
        for first, size in chunks(span):
            height = size * GROUP
            lane = lanes_of(height)
            at = pl.ds(base + first, size)
            field = (inverse[layer, at] * noise[layer, at]).reshape(height, columns)
            for t in range(tiles):
                initial[layer + 1, t, pl.ds((first + 1) * GROUP, height), :] = field[:, t * LANES : (t + 1) * LANES]
            both = jnp.where(lane == LANES - 1, field[:, columns - LANES :], field[:, :LANES])
            turned = pltpu.roll(both, layer * SLOT + 1, 1)
            here = pl.ds(first * GROUP, height)
            own[here, :] = jnp.where(lane // SLOT == layer, turned, own[here, :])
        return carry

    lax.fori_loop(0, layers, first_step, 0, unroll=unroll)

    lane = lanes_of(rows)
    place = lane % SLOT
    side = jnp.where(place < 2, own[...], packed_inverse * packed_noise)
    total = jnp.where(lane >= SLOT, pltpu.roll(side, SLOT, 1), 0.0)
    total = total + jnp.where(lane < LANES - SLOT, pltpu.roll(side, LANES - SLOT, 1), 0.0)
    total = total + pltpu.roll(side, 1, 0) + pltpu.roll(side, rows - 1, 0)
    total = total + jnp.where(
        place == 3,
        pltpu.roll(side, 1, 1) + pltpu.roll(side, 2, 1),
        pltpu.roll(side, LANES - 1, 1) + pltpu.roll(side, 4, 1),
    )
    side_middle = packed_inverse * (packed_noise + total)
    sides[...] = jnp.where(place == 2, pltpu.roll(side, LANES - 2, 1), side)
    sides_middle[...] = jnp.where(place == 2, pltpu.roll(side_middle, LANES - 2, 1), side_middle)

    def second_step(layer, carry):
        for first, size in chunks(span):
            height = size * GROUP
            at = pl.ds(base + first, size)
            totals = around(initial, sides, layer, (first + 1) * GROUP, height)
            for t in range(tiles):
                part = pl.ds(t * LANES, LANES)
                field = inverse[layer, at, :, part] * (noise[layer, at, :, part] + totals[t].reshape(size, GROUP, LANES))
                middle[layer + 1, t, pl.ds((first + 1) * GROUP, height), :] = field.reshape(height, LANES)
        return carry

    lax.fori_loop(0, layers, second_step, 0, unroll=unroll)
    wait_pivots()

    def third_step(layer, carry):
        for first, size in chunks(groups):
            height = size * GROUP
            at = pl.ds(base + 1 + first, size)
            here = pl.ds(first, size)
            totals = around(middle, sides_middle, layer, (first + 2) * GROUP, height)
            for t in range(tiles):
                part = pl.ds(t * LANES, LANES)
                field = inverse[layer, at, :, part] * (noise[layer, at, :, part] + totals[t].reshape(size, GROUP, LANES))
                pivot = pivots[layer, pl.ds(base + first, size), :, part]
                forward[layer + 1, here, :, part] = (field + forward[layer, here, :, part]) * pivot
        return carry

    lax.fori_loop(0, layers, third_step, 0, unroll=unroll)

    def last_step(step, carry):
        layer = layers - 1 - step
        for first, size in chunks(groups):
            here = pl.ds(first, size)
            pivot = pivots[layer, pl.ds(base + first, size)]
            forward[layer + 1, here] = forward[layer + 1, here] + pivot * forward[layer + 2, here]
        finished(layer)
        return carry

    lax.fori_loop(0, layers, last_step, 0, unroll=unroll)


def solve_scratch(layers, groups, columns):
    block = functools.partial(pltpu.VMEM, dtype=jnp.float32)
    padded = (layers + 2, columns // LANES, (groups + 4) * GROUP, LANES)
    rows = (groups + 2) * GROUP
    return [
        block(padded),
        block(padded),
        block((layers + 2, groups, GROUP, columns)),
        block((rows, LANES)),
        block((rows, LANES)),
        block((rows, LANES)),
    ]


def merged_sides(paired, other):
    odd = lax.axis_index("ay") % 2
    is_left = (lanes_of(paired.shape[0]) % SLOT < 4).astype(jnp.int32)
    return jnp.where(is_left == odd, paired, other)


def last_two(half):
    me = lax.axis_index("ay")
    one, other = me ^ half, me ^ (half + 1)
    return jnp.minimum(one, other), one, other


def block_kernel(half, depth, *refs):
    known = 2 * half - 3
    inverse_in, pivots_in, own_piece, own_sides = refs[:4]
    pieces = refs[4 : 4 + known]
    paired, other, above, below = refs[4 + known : 8 + known]
    out, noise_out, inverse_out, pivots_out, packed_noise, packed_inverse = refs[8 + known : 14 + known]
    noise, inverse, pivots, thin, *scratch, sems, out_sems = refs[14 + known :]
    initial, middle, forward, own, sides, sides_middle = scratch
    layers, groups, _, columns = pivots_in.shape
    rows, height, lines = depth * GROUP, groups * GROUP, thin.shape[1]
    me = lax.axis_index("ay")
    last = last_two(half)[0] * depth
    steps = [0] + [step for step in range(2 * half - 1, 0, -1) if step not in (half, half + 1)]

    inverse_copy = pltpu.make_async_copy(inverse_in, inverse.at[:, pl.ds(2, groups)], sems.at[0])
    pivot_copy = pltpu.make_async_copy(pivots_in, pivots.at[:, pl.ds(1, groups)], sems.at[1])
    waits, thin_copies = [inverse_copy], []
    inverse_copy.start()
    for index, step in enumerate(steps):
        target = noise.at[:, pl.ds(2 + (me ^ step) * depth, depth)]
        if step:
            message = pieces[index - 1]
            piece = strip_of(message, layers, depth)
            side = message.at[pl.ds(layers * depth, lines)]
        else:
            piece = own_piece.at[:, :, :, pl.ds(pl.multiple_of(me * columns, LANES), columns)]
            side = own_sides
        waits.append(pltpu.make_async_copy(piece, target, sems.at[2 + index]))
        waits[-1].start()
        thin_copies.append(pltpu.make_async_copy(side, thin.at[index], sems.at[2 + len(steps) + index]))
        thin_copies[-1].start()
    pivot_copy.start()

    nothing = jnp.zeros((layers, GROUP, columns), jnp.float32)
    for ref in (noise, inverse):
        for group in (0, 1, groups + 2, groups + 3):
            ref[:, group] = nothing
    pivots[:, 0] = nothing
    pivots[:, groups + 1] = nothing
    packed_noise[...] = jnp.zeros(packed_noise.shape, jnp.float32)
    packed_inverse[...] = jnp.zeros(packed_inverse.shape, jnp.float32)
    packed_inverse[2 * GROUP : 2 * GROUP + height] = merged_sides(paired[...], other[...])
    end = 4 * layers
    for message, group, place, row in ((above, 1, GROUP - 2, 2 * GROUP - 1), (below, groups + 2, 0, 2 * GROUP + height)):
        for layer in range(layers):
            noise[layer, group, place : place + 2, :] = message[2 * layer : 2 * layer + 2, :]
            inverse[layer, group, place : place + 2, :] = message[2 * (layers + layer) : 2 * (layers + layer) + 2, :]
        packed_noise[row : row + 1] = message[end : end + 1, :LANES]
        packed_inverse[row : row + 1] = message[end : end + 1, LANES : 2 * LANES]
    for index, step in enumerate(steps):
        thin_copies[index].wait()
        unfold_into(packed_noise, 2 * GROUP + (me ^ step) * rows, thin.at[index], rows)
    for copy in waits:
        copy.wait()
    windows = [
        pltpu.make_async_copy(noise.at[:, pl.ds(last, 2)], noise_out.at[:, pl.ds(0, 2)], sems.at[0]),
        pltpu.make_async_copy(noise.at[:, pl.ds(last + 2 * depth + 2, 2)], noise_out.at[:, pl.ds(2, 2)], sems.at[2]),
        pltpu.make_async_copy(inverse.at[:, pl.ds(last, 2 * depth + 4)], inverse_out, sems.at[3]),
    ]
    for copy in windows:
        copy.start()
    pivot_window = pltpu.make_async_copy(pivots.at[:, pl.ds(last, 2 * depth + 2)], pivots_out, sems.at[6])

    def wait_pivots():
        pivot_copy.wait()
        pivot_window.start()

    def place_out(layer):
        return pltpu.make_async_copy(forward.at[layer + 1], out.at[layer], out_sems.at[layer])

    inner = pl.ds(GROUP, height + 2 * GROUP)
    solve(
        noise, inverse, pivots, 1, packed_noise[inner, :], packed_inverse[inner, :],
        initial, middle, forward, (own, sides, sides_middle), wait_pivots, lambda layer: place_out(layer).start(),
    )
    for layer in range(layers):
        place_out(layer).wait()
    for copy in windows:
        copy.wait()
    pivot_window.wait()


def solve_block(inverse, pivots, own_piece, own_sides, pieces, paired, other, above, below, half, depth):
    layers, groups, _, columns = pivots.shape
    block = functools.partial(pltpu.VMEM, dtype=jnp.float32)
    packed = f32((groups + 4) * GROUP, LANES)
    return pl.pallas_call(
        functools.partial(block_kernel, half, depth),
        in_specs=[ANYWHERE] * (4 + len(pieces)) + [WHOLE] * 4,
        out_specs=[ANYWHERE] * 4 + [WHOLE] * 2,
        out_shape=[
            f32(layers, groups, GROUP, columns),
            f32(layers, 4, GROUP, columns),
            f32(layers, 2 * depth + 4, GROUP, columns),
            f32(layers, 2 * depth + 2, GROUP, columns),
            packed,
            packed,
        ],
        scratch_shapes=[
            block((layers, groups + 4, GROUP, columns)),
            block((layers, groups + 4, GROUP, columns)),
            block((layers, groups + 2, GROUP, columns)),
            block((len(pieces) + 1, *own_sides.shape)),
            *solve_scratch(layers, groups, columns),
            pltpu.SemaphoreType.DMA((2 * len(pieces) + 7,)),
            pltpu.SemaphoreType.DMA((layers,)),
        ],
        compiler_params=pltpu.CompilerParams(vmem_limit_bytes=40 * MIB),
    )(inverse, pivots, own_piece, own_sides, *pieces, paired, other, above, below)


def edge_kernel(steps, count, own_piece, own_sides, inverse, paired, other, *refs):
    pieces, tips = refs[: len(steps) - 1], refs[len(steps) - 1 : len(steps) + 1]
    up, down, ends, thin, outer, sems = refs[len(steps) + 1 :]
    layers, columns = ends.shape[1], ends.shape[3]
    depth, lines = own_piece.shape[1], thin.shape[1]
    height = paired.shape[0]
    half = count // 2
    wide = columns // LANES
    me = lax.axis_index("ay")
    copies = [
        pltpu.make_async_copy(inverse.at[:, 0], outer.at[0], sems.at[0]),
        pltpu.make_async_copy(inverse.at[:, inverse.shape[1] - 1], outer.at[1], sems.at[1]),
    ]
    for copy in copies:
        copy.start()

    def fetch(step, piece, side):
        if step:
            rows, sides = strip_of(piece, layers, depth), piece.at[pl.ds(layers * depth, lines)]
        else:
            rows, sides = own_piece.at[:, :, :, pl.ds(pl.multiple_of(me * columns, LANES), columns)], own_sides
        pltpu.make_async_copy(rows.at[:, side * (depth - 1)], ends.at[side], sems.at[2 + side]).start()
        pltpu.make_async_copy(sides, thin.at[side], sems.at[4 + side]).start()

    for step, piece in zip(steps, (None, *pieces)):
        for side in range(2):
            pl.when((me ^ step) == side * (count - 1))(functools.partial(fetch, step, piece, side))
    for copy in copies:
        copy.wait()
    for side, (out, place, row) in enumerate(((up, 0, 0), (down, GROUP - 2, height - 1))):
        target = side * (count - 1)
        late = ((me ^ half) == target) | ((me ^ (half + 1)) == target)

        def wait(side):
            pltpu.make_async_copy(ends.at[side], ends.at[side], sems.at[2 + side]).wait()
            pltpu.make_async_copy(thin.at[side], thin.at[side], sems.at[4 + side]).wait()

        pl.when(jnp.logical_not(late))(functools.partial(wait, side))
        tip = jnp.where((me ^ half) == target, tips[0][: 2 * layers + GROUP], tips[1][...])
        for layer in range(layers):
            out[2 * layer : 2 * layer + 2, :] = jnp.where(
                late, tip[2 * layer : 2 * layer + 2, :], ends[side, layer, place : place + 2, :]
            )
            out[2 * (layers + layer) : 2 * (layers + layer) + 2, :] = outer[side, layer, place : place + 2, :]
        if side:
            i = depth // 2 - 1
            both = thin[side, i // wide, :, i % wide * LANES : (i % wide + 1) * LANES]
            corner = pltpu.roll(both, LANES - 4, 1)[GROUP - 1 :]
        else:
            corner = thin[side, 0, 0:1, :LANES]
        end = 4 * layers
        out[end : end + GROUP, :] = jnp.zeros((GROUP, columns), jnp.float32)
        out[end : end + 1, :LANES] = jnp.where(late, tip[2 * layers : 2 * layers + 1, :LANES], corner)
        out[end : end + 1, LANES : 2 * LANES] = merged_sides(paired[row : row + 1, :], other[row : row + 1, :])


def edges(own_piece, own_sides, inverse, paired, other, steps, pieces, tips, count):
    layers, _, _, columns = inverse.shape
    outer = f32(4 * layers + GROUP, columns)
    block = functools.partial(pltpu.VMEM, dtype=jnp.float32)
    return pl.pallas_call(
        functools.partial(edge_kernel, steps, count),
        in_specs=[ANYWHERE] * 3 + [WHOLE] * 2 + [ANYWHERE] * len(pieces) + [WHOLE] * 2,
        out_specs=[WHOLE] * 2,
        out_shape=[outer, outer],
        scratch_shapes=[
            block((2, layers, GROUP, columns)),
            block((2, *own_sides.shape)),
            block((2, layers, GROUP, columns)),
            pltpu.SemaphoreType.DMA((6,)),
        ],
        compiler_params=pltpu.CompilerParams(vmem_limit_bytes=12 * MIB),
    )(own_piece, own_sides, inverse, paired, other, *pieces, *tips)


def tail_kernel(half, depth, known, inverse_in, pivots_in, packed_noise, packed_inverse, before, lower, upper, partial, out, noise, inverse, pivots, packed, thin, *rest):
    del partial
    initial, middle, forward, own, sides, sides_middle, sems, out_sems = rest
    layers, groups, _, columns = pivots.shape
    count = 2 * half
    last, one, other = last_two(half)
    part = lower.shape[0] // depth
    lines = thin.shape[1]
    at_one, at_other = (pl.ds(2 + (strip - last) * depth, depth) for strip in (one, other))
    copies = [
        pltpu.make_async_copy(strip_of(upper, layers - part, depth), noise.at[pl.ds(part, layers - part), at_one], sems.at[0]),
        pltpu.make_async_copy(strip_of(lower, part, depth), noise.at[pl.ds(0, part), at_one], sems.at[1]),
        pltpu.make_async_copy(strip_of(before, layers, depth), noise.at[:, at_other], sems.at[2]),
        pltpu.make_async_copy(known.at[:, pl.ds(0, 2)], noise.at[:, pl.ds(0, 2)], sems.at[3]),
        pltpu.make_async_copy(known.at[:, pl.ds(2, 2)], noise.at[:, pl.ds(2 * depth + 2, 2)], sems.at[4]),
        pltpu.make_async_copy(inverse_in, inverse, sems.at[6]),
        pltpu.make_async_copy(upper.at[pl.ds((layers - part) * depth, lines)], thin.at[0], sems.at[7]),
        pltpu.make_async_copy(before.at[pl.ds(layers * depth, lines)], thin.at[1], sems.at[8]),
    ]
    pivot_copy = pltpu.make_async_copy(pivots_in, pivots, sems.at[5])
    for copy in (*copies, pivot_copy):
        copy.start()
    inner = pl.ds(pl.multiple_of(last * depth * GROUP, GROUP), (groups + 2) * GROUP)
    packed[...] = packed_noise[inner, :]
    for copy in copies:
        copy.wait()
    for index, strip in enumerate((one, other)):
        unfold_into(packed, (2 + (strip - last) * depth) * GROUP, thin.at[index], depth * GROUP)

    def place_out(layer):
        return pltpu.make_async_copy(
            forward.at[layer + 1, pl.ds(1, 2 * depth)], out.at[layer, pl.ds(last * depth, 2 * depth)], out_sems.at[layer]
        )

    solve(
        noise, inverse, pivots, 0, packed[...], packed_inverse[inner, :],
        initial, middle, forward, (own, sides, sides_middle), pivot_copy.wait, lambda layer: place_out(layer).start(), layers,
    )

    def edge(own_group, to, sem):
        return pltpu.make_async_copy(forward.at[pl.ds(1, layers), pl.ds(own_group, 1)], out.at[:, pl.ds(to, 1)], sem)

    above = edge(0, jnp.maximum(last * depth - 1, 0), sems.at[0])
    below = edge(groups - 1, jnp.minimum((last + 2) * depth, count * depth - 1), sems.at[1])
    pl.when(last > 0)(above.start)
    pl.when(last < count - 2)(below.start)
    for layer in range(layers):
        place_out(layer).wait()
    pl.when(last > 0)(above.wait)
    pl.when(last < count - 2)(below.wait)


def solve_tail(sides, inverse, pivots, packed_noise, packed_inverse, before, lower, upper, partial, half, depth):
    layers, groups, _, columns = pivots.shape
    block = functools.partial(pltpu.VMEM, dtype=jnp.float32)
    return pl.pallas_call(
        functools.partial(tail_kernel, half, depth),
        in_specs=[ANYWHERE] * 3 + [WHOLE] * 2 + [ANYWHERE] * 4,
        out_specs=ANYWHERE,
        out_shape=f32(*partial.shape),
        scratch_shapes=[
            block((layers, groups + 2, GROUP, columns)),
            block((layers, groups + 2, GROUP, columns)),
            block((layers, groups, GROUP, columns)),
            block(((groups + 2) * GROUP, LANES)),
            block((2, before.shape[0] - layers * depth, GROUP, columns)),
            *solve_scratch(layers, groups, columns),
            pltpu.SemaphoreType.DMA((9,)),
            pltpu.SemaphoreType.DMA((layers,)),
        ],
        input_output_aliases={8: 0},
        compiler_params=pltpu.CompilerParams(vmem_limit_bytes=20 * MIB),
    )(sides, inverse, pivots, packed_noise, packed_inverse, before, lower, upper, partial)


def after(cells, *tokens):
    return lax.optimization_barrier((cells, *tokens))[0]


def body(noise, kappa, mask):
    layers, rows, width = noise.shape
    count = lax.axis_size("ay")
    across = lax.axis_size("ax")
    half = count // 2
    depth = rows // GROUP

    def swap(cells, step):
        return lax.ppermute(cells, "ay", [(i, i ^ step) for i in range(count)])

    def grouped(cells):
        return cells.reshape(layers, -1, GROUP, cells.shape[2])

    noise = grouped(noise)
    part = layers // 4
    first, own, split = count - 1, 0, half
    specs = {first: (first, 0, layers, True)}
    for step in [*range(count - 2, half, -1), *range(half - 1, 0, -1)]:
        specs[step] = (step, 0, layers, True)
    specs["lower"], specs["upper"] = (split, 0, part, False), (split, part, layers - part, True)
    specs[own] = (own, 0, 0, True)
    parts = {first: messages(noise, (specs.pop(first),), count)[0]}
    late = (half, half + 1)
    *made, tip = messages(after(noise, parts[first]), tuple(specs.values()), count, late)
    parts.update(zip(specs, made))
    inverse, pivots, packed = coefficients(after(kappa, parts[first]), mask)

    got = {first: swap(parts[first], first)}
    between = [pair for i in range(1, count - 1, 2) for pair in ((i, i + 1), (i + 1, i))]
    tip = lax.ppermute(tip, "ay", [(0, half), (count - 1, half - 1)])
    handed = swap(tip[tip.shape[0] // 2 :], 1)
    paired = swap(packed, 1)
    other = lax.ppermute(packed, "ay", between)
    for step in range(count - 2, half + 1, -1):
        got[step] = swap(after(parts[step], paired), step)
    got[half + 1] = swap(after(parts[half + 1], other, handed), half + 1)
    for step in range(half - 1, 1, -1):
        got[step] = swap(after(parts[step], other, handed), step)
    got[1] = swap(after(parts[1], got[first]), 1)
    lower = swap(after(parts["lower"], got[half + 2]), split)
    upper = swap(after(parts["upper"], got[half + 2]), split)
    inverse, pivots = grouped(inverse), grouped(pivots)

    steps = (0, *(step for step in range(count - 1, 0, -1) if step not in late))
    up, down = edges(
        noise, parts[0], inverse, paired, other, steps, [got[step] for step in steps[1:]], (tip, handed), count
    )
    above = lax.ppermute(down, "ax", [(i, i + 1) for i in range(across - 1)])
    below = lax.ppermute(up, "ax", [(i + 1, i) for i in range(across - 1)])
    partial, noise_part, inverse_part, pivots_part, packed_noise, packed_inverse = solve_block(
        inverse, pivots, noise, parts[0], [got[step] for step in steps[1:]], paired, other, above, below, half, depth
    )
    sample = solve_tail(
        noise_part, inverse_part, pivots_part, packed_noise, packed_inverse, got[half + 1], lower, upper, partial, half, depth
    )
    return sample.reshape(layers, rows * count, -1)


def solution(mesh):
    in_specs = (P(None, ("ax", "ay"), None), P(None, "ax", "ay"), P("ax", "ay"))
    out_specs = P(None, "ax", "ay")
    return jax.shard_map(body, mesh=mesh, in_specs=in_specs, out_specs=out_specs, check_vma=False)
```
